128 devices in a mesh: batch: 16 (over x, y_hi, core), replica: 8 (over z, y_lo).
Axes of the slice: x: 4, y: 4 (y_hi: 2, y_lo: 2; y = y_hi * 2 + y_lo), z: 4, core: 2. Of those that a mesh axis runs over, the one named last changes fastest.
Arguments:
- sensor_feats: bfloat16 [40960, 1024], P(('batch', 'replica')), may hold values from -6 to 6
- proj_weight: bfloat16 [1024, 1024], replicated, may hold values from -0.1875 to 0.1875
- text_feats: bfloat16 [40960, 1024], P(('batch', 'replica')), may hold values from -0.29882812 to 0.29882812
Outputs:
- text_grad: float32 [40960, 1024], P(('batch', 'replica'))
- weight_grad: float32 [1024, 1024], P('batch')
The draws below stay inside these ranges and needn't reach their ends.
All inputs are finite; a program needn't handle non-finite values.
Results may differ from the reference program's by a relative error of at most 0.0051.
Values may be sent and summed in bfloat16 or wider, within the bound.
No kernel may reach another device: no remote copies, remote signals or barrier semaphores. Data moves between devices by JAX's collectives and lax.ppermute only.
A program may use at most 128 MiB of HBM per device.

```python
import jax
import jax.numpy as jnp
from jax import lax

D = 1024
E = 1024
B_DEV = 320
TOKENS = 40960
N_BATCH = 16
N_REPLICA = 8


def steps_of(stream_key, shape, cuts, smallest, largest):
    def one(dim, shards_of):
        heights = jax.random.uniform(jax.random.fold_in(jax.random.fold_in(stream_key, 6), dim), (shards_of,), jnp.float32, smallest / len(cuts), largest / len(cuts))
        return jnp.repeat(jnp.exp(heights), shape[dim] // shards_of).reshape((-1,) + (1,) * (len(shape) - dim - 1))

    loudness = one(*cuts[0])
    for cut in cuts[1:]:
        loudness = loudness * one(*cut)
    return loudness


def bell_draw(rng, extent, scale, most, split=(), kind=jnp.bfloat16):
    array = scale * jax.random.normal(rng, extent, jnp.float32)
    if split:
        array = array * steps_of(rng, extent, split, -0.22, 0.18)
    return jnp.clip(array, -most, most).astype(kind)


def setup_inputs(seed: int = 0) -> dict:
    keys = jax.random.split(jax.random.key(seed), 4)
    return {
        "sensor_feats": bell_draw(keys[0], (TOKENS, D), 1.0, 6.0, ((0, 128),)),
        "proj_weight": bell_draw(keys[1], (D, E), D ** -0.5, 0.1875),
        "text_feats": bell_draw(keys[2], (TOKENS, E), 0.05, 0.29882812, ((0, 128),)),
    }


LOGIT_SCALE = 10.0
LOGIT_BIAS = -2.0
EPSILON = 1e-06

def normalize(values):
    length = jnp.sqrt(lax.optimization_barrier(jnp.sum(values * values, axis=-1, keepdims=True)) + EPSILON)
    return (values / length, length)

def group_grads(sensor_unit, text_unit):
    group_rows = sensor_unit.shape[0]
    sensor_blocks = sensor_unit.reshape(N_BATCH, B_DEV, E)
    offsets = jnp.arange(N_BATCH, dtype=jnp.int32) * B_DEV
    columns = jnp.arange(group_rows, dtype=jnp.int32)

    def visit(text_part, inputs):
        sensor_block, offset = inputs
        logits = LOGIT_SCALE * jnp.dot(sensor_block, text_unit.T, preferred_element_type=jnp.float32) + LOGIT_BIAS
        row_ids = offset + jnp.arange(B_DEV, dtype=jnp.int32)
        positive = (row_ids[:, None] == columns[None, :]).astype(jnp.float32)
        slopes = (jax.nn.sigmoid(logits) - positive).astype(jnp.bfloat16)
        block_grad = LOGIT_SCALE * jnp.dot(slopes, text_unit, preferred_element_type=jnp.float32)
        text_part = text_part + LOGIT_SCALE * jnp.dot(slopes.T, sensor_block, preferred_element_type=jnp.float32)
        return (text_part, block_grad)
    text_part, sensor_grad = lax.scan(visit, jnp.zeros((group_rows, E), jnp.float32), (sensor_blocks, offsets))
    return (sensor_grad.reshape(group_rows, E), text_part)

def to_groups(values):
    return values.reshape(N_BATCH, N_REPLICA, B_DEV, E).transpose(1, 0, 2, 3).reshape(N_REPLICA, N_BATCH * B_DEV, E)

def from_groups(values):
    return values.reshape(N_REPLICA, N_BATCH, B_DEV, E).transpose(1, 0, 2, 3).reshape(TOKENS, E)

def reference(sensor_feats, proj_weight, text_feats):
    sensor_raw = jnp.dot(sensor_feats, proj_weight, preferred_element_type=jnp.float32)
    sensor_norm, sensor_len = normalize(sensor_raw)
    text_norm, text_len = normalize(text_feats.astype(jnp.float32))
    sensor_unit = sensor_norm.astype(jnp.bfloat16)
    text_unit = text_norm.astype(jnp.bfloat16)

    def per_group(pair):
        return group_grads(pair[0], pair[1])
    sensor_grad, text_part = lax.map(per_group, (to_groups(sensor_unit), to_groups(text_unit)))
    sensor_grad = from_groups(sensor_grad)
    text_part = from_groups(text_part)
    text_grad = (text_part - text_norm * lax.optimization_barrier(jnp.sum(text_norm * text_part, axis=-1, keepdims=True))) / text_len
    raw_grad = ((sensor_grad - sensor_norm * lax.optimization_barrier(jnp.sum(sensor_norm * sensor_grad, axis=-1, keepdims=True))) / sensor_len).astype(jnp.bfloat16)
    weight_grad = jnp.dot(sensor_feats.T, raw_grad, preferred_element_type=jnp.float32)
    return (text_grad, weight_grad)
```

```python
import itertools

import jax
import jax.numpy as jnp
from jax import lax
from jax.sharding import Mesh, PartitionSpec as P

LOGIT_SCALE = 10.0
LOGIT_BIAS = -2.0
EPSILON = 1e-06

SIZES = (4, 2, 2, 4, 2)
AXES = ("x", "yh", "c", "z", "yl")
F32 = jnp.float32
BF16 = jnp.bfloat16


def position(coords):
    index = 0
    for size, coord in zip(SIZES, coords):
        index = index * size + coord % size
    return index


def send(block, **shift):
    step = [shift.get(name, 0) for name in AXES]
    route = [
        (position(at), position([a + s for a, s in zip(at, step)]))
        for at in itertools.product(*map(range, SIZES))
    ]
    return lax.ppermute(block, AXES, route)


def normalize(values):
    length = jnp.sqrt(jnp.sum(values * values, axis=-1, keepdims=True) + EPSILON)
    return (values / length, length)


def project(grad, norm, length):
    return (grad - norm * jnp.sum(norm * grad, axis=-1, keepdims=True)) / length


def sensor_part(feats, proj_weight, texts, diagonal):
    raw = jnp.dot(feats, proj_weight, preferred_element_type=F32)
    norm, length = normalize(raw)
    unit = norm.astype(BF16)
    logits = LOGIT_SCALE * jnp.dot(unit, texts.T, preferred_element_type=F32) + LOGIT_BIAS
    slopes = jax.nn.sigmoid(logits)
    if diagonal:
        rows = lax.broadcasted_iota(jnp.int32, slopes.shape, 0)
        columns = lax.broadcasted_iota(jnp.int32, slopes.shape, 1)
        slopes = slopes - (rows == columns).astype(F32)
    slopes = slopes.astype(BF16)
    grad = LOGIT_SCALE * jnp.dot(slopes, texts, preferred_element_type=F32)
    return unit, slopes, project(grad, norm, length).astype(BF16)


def local(sensor_feats, proj_weight, text_feats):
    rows = sensor_feats.shape[0]
    half = rows // 2
    text_y = send(text_feats, yh=1)
    text_c = send(text_feats, c=1)
    low, high = sensor_feats[:half], sensor_feats[half:]
    right_low = send(low, x=1)
    left_high = send(high, x=-1)
    right_high = send(high, x=1)
    left_low = send(low, x=-1)
    far_low = send(right_low, x=1)
    far_high = send(left_high, x=-1)
    text_yc = send(text_y, c=1)

    text_norm, text_len = normalize(text_feats.astype(F32))
    y_norm, y_len = normalize(text_y.astype(F32))
    texts = jnp.concatenate(
        [
            text_norm.astype(BF16),
            y_norm.astype(BF16),
            normalize(text_c.astype(F32))[0].astype(BF16),
            normalize(text_yc.astype(F32))[0].astype(BF16),
        ]
    )
    feats = [
        sensor_feats,
        jnp.concatenate([right_low, right_high]),
        jnp.concatenate([left_low, left_high]),
        jnp.concatenate([far_low, far_high]),
    ]
    parts = [sensor_part(f, proj_weight, texts, k == 0) for k, f in enumerate(feats)]
    units, slopes, raw_grads = (jnp.concatenate(p) for p in zip(*parts))
    feats = jnp.concatenate(feats)

    core = lax.axis_index("c")
    weight_part = jnp.dot(feats.T, raw_grads, preferred_element_type=F32)
    weight_part = weight_part.reshape(8, 2, 64, weight_part.shape[1])
    mine = jnp.where(core == 0, weight_part[:, 0], weight_part[:, 1])
    other = jnp.where(core == 0, weight_part[:, 1], weight_part[:, 0])
    weight_sum = (mine + send(other.astype(BF16), c=1).astype(F32)).astype(BF16)

    text_part = LOGIT_SCALE * jnp.dot(slopes.T, units, preferred_element_type=F32)
    text_sum = text_part[: 2 * rows] + send(text_part[2 * rows :], c=1)
    text_out = send(project(text_sum[rows:], y_norm, y_len).astype(BF16), yh=1)

    weight_all = lax.all_to_all(weight_sum, ("x", "yh"), split_axis=0, concat_axis=0, tiled=True)
    weight_sum = jnp.sum(weight_all.astype(F32), axis=0).astype(BF16)
    across = send(weight_sum, z=2)
    ahead, behind = send(weight_sum, z=1), send(weight_sum, z=-1)
    weight_sum = (
        (weight_sum.astype(F32) + across.astype(F32)) + (ahead.astype(F32) + behind.astype(F32))
    ).astype(BF16)
    weight_grad = weight_sum.astype(F32) + send(weight_sum, yl=1).astype(F32)

    text_grad = project(text_sum[:rows], text_norm, text_len) + text_out.astype(F32)
    return (text_grad, weight_grad)


def solution(mesh):
    fine = Mesh(mesh.devices.reshape(SIZES), AXES)
    return jax.shard_map(
        local,
        mesh=fine,
        in_specs=(P(AXES, None), P(), P(AXES, None)),
        out_specs=(P(AXES, None), P(("x", "yh", "c"), None)),
        check_vma=False,
    )
```

```python
import functools
import itertools

import jax
import jax.numpy as jnp
from jax import lax
from jax.experimental import pallas as pl
from jax.experimental.pallas import tpu as pltpu
from jax.sharding import Mesh, PartitionSpec as P

LOGIT_SCALE = 10.0
LOGIT_BIAS = -2.0
EPSILON = 1e-06

SIZES = (4, 2, 2, 4, 2)
AXES = ("x", "yh", "c", "z", "yl")
F32 = jnp.float32
BF16 = jnp.bfloat16


def position(coords):
    index = 0
    for size, coord in zip(SIZES, coords):
        index = index * size + coord % size
    return index


def send(block, **shift):
    step = [shift.get(name, 0) for name in AXES]
    route = [
        (position(at), position([a + s for a, s in zip(at, step)]))
        for at in itertools.product(*map(range, SIZES))
    ]
    return lax.ppermute(block, AXES, route)


def normalize(values):
    length = jnp.sqrt(jnp.sum(values * values, axis=-1, keepdims=True) + EPSILON)
    return (values / length, length)


def project(grad, norm, length):
    return (grad - norm * jnp.sum(norm * grad, axis=-1, keepdims=True)) / length


def sensor_kernel(diagonal, feats, proj_weight, texts, unit_out, slopes_out, raw_grad_out):
    raw = jnp.dot(feats[...], proj_weight[...], preferred_element_type=F32)
    norm, length = normalize(raw)
    unit = norm.astype(BF16)
    unit_out[...] = unit
    logits = LOGIT_SCALE * jnp.dot(unit, texts[...].T, preferred_element_type=F32) + LOGIT_BIAS
    slopes = jax.nn.sigmoid(logits)
    if diagonal:
        rows = lax.broadcasted_iota(jnp.int32, slopes.shape, 0)
        columns = lax.broadcasted_iota(jnp.int32, slopes.shape, 1)
        slopes = slopes - (rows == columns).astype(F32)
    slopes = slopes.astype(BF16)
    slopes_out[...] = slopes
    grad = LOGIT_SCALE * jnp.dot(slopes, texts[...], preferred_element_type=F32)
    raw_grad_out[...] = project(grad, norm, length).astype(BF16)


def sensor_part(feats, proj_weight, texts, diagonal):
    rows, depth = feats.shape
    width, columns = proj_weight.shape[1], texts.shape[0]
    whole = pl.BlockSpec(memory_space=pltpu.VMEM)
    return pl.pallas_call(
        functools.partial(sensor_kernel, diagonal),
        out_shape=(
            jax.ShapeDtypeStruct((rows, width), BF16),
            jax.ShapeDtypeStruct((rows, columns), BF16),
            jax.ShapeDtypeStruct((rows, width), BF16),
        ),
        in_specs=[whole] * 3,
        out_specs=(whole,) * 3,
        compiler_params=pltpu.CompilerParams(vmem_limit_bytes=40 * 1024 * 1024),
        cost_estimate=pl.CostEstimate(
            flops=2 * rows * width * (depth + 2 * columns),
            bytes_accessed=2 * (rows * (depth + 2 * width + columns) + (depth + columns) * width),
            transcendentals=rows * columns,
        ),
    )(feats, proj_weight, texts)


def local(sensor_feats, proj_weight, text_feats):
    rows = sensor_feats.shape[0]
    half = rows // 2
    right, left = send(sensor_feats, x=1), send(sensor_feats, x=-1)
    text_y, text_c = send(text_feats, yh=1), send(text_feats, c=1)
    text_norm, text_len = normalize(text_feats.astype(F32))
    c_unit = normalize(text_c.astype(F32))[0].astype(BF16)
    far_low, far_high = send(right[:half], x=1), send(left[half:], x=-1)
    text_yc = send(text_y, c=1)
    y_norm, y_len = normalize(text_y.astype(F32))
    yc_unit = normalize(text_yc.astype(F32))[0].astype(BF16)
    texts = jnp.concatenate([text_norm.astype(BF16), y_norm.astype(BF16), c_unit, yc_unit])

    feats = [sensor_feats, right, left]
    parts = [sensor_part(f, proj_weight, texts, k == 0) for k, f in enumerate(feats)]
    parts, far_low, far_high = lax.optimization_barrier((parts, far_low, far_high))
    feats.append(jnp.concatenate([far_low, far_high]))
    parts.append(sensor_part(feats[-1], proj_weight, texts, False))
    units, slopes, raw_grads = (jnp.concatenate(p) for p in zip(*parts))
    feats = jnp.concatenate(feats)

    core = lax.axis_index("c")
    weight_part = jnp.dot(feats.T, raw_grads, preferred_element_type=F32)
    weight_part = weight_part.reshape(8, 2, 64, weight_part.shape[1])
    mine = jnp.where(core == 0, weight_part[:, 0], weight_part[:, 1])
    other = jnp.where(core == 0, weight_part[:, 1], weight_part[:, 0]).astype(BF16)
    other, units, slopes = lax.optimization_barrier((other, units, slopes))
    weight_recv = send(other, c=1)
    text_part = LOGIT_SCALE * jnp.dot(slopes.T, units, preferred_element_type=F32)
    weight_recv, text_part = lax.optimization_barrier((weight_recv, text_part))
    weight_sum = (mine + weight_recv.astype(F32)).astype(BF16)

    text_recv = send(text_part[2 * rows :], c=1)
    weight_all = lax.all_to_all(weight_sum, ("x", "yh"), split_axis=0, concat_axis=0, tiled=True)
    text_sum = text_part[: 2 * rows] + text_recv
    text_send = project(text_sum[rows:], y_norm, y_len).astype(BF16)
    text_out = send(text_send, yh=1)
    weight_sum = jnp.sum(weight_all.astype(F32), axis=0).astype(BF16)
    across = send(weight_sum, z=2)
    ahead, behind = send(weight_sum, z=1), send(weight_sum, z=-1)
    weight_sum = (
        (weight_sum.astype(F32) + across.astype(F32)) + (ahead.astype(F32) + behind.astype(F32))
    ).astype(BF16)
    weight_sum, text_out = lax.optimization_barrier((weight_sum, text_out))
    weight_grad = weight_sum.astype(F32) + send(weight_sum, yl=1).astype(F32)

    text_grad = project(text_sum[:rows], text_norm, text_len) + text_out.astype(F32)
    return (text_grad, weight_grad)


def solution(mesh):
    fine = Mesh(mesh.devices.reshape(SIZES), AXES)
    return jax.shard_map(
        local,
        mesh=fine,
        in_specs=(P(AXES, None), P(), P(AXES, None)),
        out_specs=(P(AXES, None), P(("x", "yh", "c"), None)),
        check_vma=False,
    )
```

```python
import functools
import itertools

import jax
import jax.numpy as jnp
from jax import lax
from jax.experimental import pallas as pl
from jax.experimental.pallas import tpu as pltpu
from jax.sharding import Mesh, PartitionSpec as P

LOGIT_SCALE = 10.0
LOGIT_BIAS = -2.0
EPSILON = 1e-06

SIZES = (4, 2, 2, 4, 2)
AXES = ("x", "yh", "c", "z", "yl")
F32 = jnp.float32
BF16 = jnp.bfloat16


def position(coords):
    index = 0
    for size, coord in zip(SIZES, coords):
        index = index * size + coord % size
    return index


def send(block, **shift):
    step = [shift.get(name, 0) for name in AXES]
    route = [
        (position(at), position([a + s for a, s in zip(at, step)]))
        for at in itertools.product(*map(range, SIZES))
    ]
    return lax.ppermute(block, AXES, route)


def normalize(values):
    length = jnp.sqrt(jnp.sum(values * values, axis=-1, keepdims=True) + EPSILON)
    return (values / length, length)


def project(grad, norm, length):
    return (grad - norm * jnp.sum(norm * grad, axis=-1, keepdims=True)) / length


def slopes_of(unit, texts, diagonal):
    logits = LOGIT_SCALE * jnp.dot(unit, texts.T, preferred_element_type=F32) + LOGIT_BIAS
    slopes = jax.nn.sigmoid(logits)
    if diagonal:
        rows = lax.broadcasted_iota(jnp.int32, slopes.shape, 0)
        columns = lax.broadcasted_iota(jnp.int32, slopes.shape, 1)
        slopes = slopes - (rows == columns).astype(F32)
    return slopes.astype(BF16)


def unit_kernel(first, second, out):
    rows = first.shape[0]
    out[:rows] = normalize(first[...].astype(F32))[0].astype(BF16)
    out[rows:] = normalize(second[...].astype(F32))[0].astype(BF16)


def stacked(refs):
    blocks = [ref[...] for ref in refs]
    return blocks[0] if len(blocks) == 1 else jnp.concatenate(blocks)


def early_kernel(count, diagonal, *refs):
    feats, (proj_weight, texts) = refs[:count], refs[count : count + 2]
    unit_out, norm_out, length_out, slopes_out, grad_out = refs[count + 2 :]
    raw = jnp.dot(stacked(feats), proj_weight[...], preferred_element_type=F32)
    norm, length = normalize(raw)
    unit = norm.astype(BF16)
    unit_out[...], norm_out[...], length_out[...] = unit, norm, length
    slopes = slopes_of(unit, texts[...], diagonal)
    slopes_out[...] = slopes
    grad_out[...] = jnp.dot(slopes, texts[...], preferred_element_type=F32)


def whole_block(feats, proj_weight, texts_a, texts_b):
    raw = jnp.dot(feats, proj_weight[...], preferred_element_type=F32)
    norm, length = normalize(raw)
    unit = norm.astype(BF16)
    slopes_a = slopes_of(unit, texts_a[...], False)
    slopes_b = slopes_of(unit, texts_b[...], False)
    grad = jnp.dot(slopes_a, texts_a[...], preferred_element_type=F32)
    grad = grad + jnp.dot(slopes_b, texts_b[...], preferred_element_type=F32)
    return unit, slopes_a, slopes_b, project(LOGIT_SCALE * grad, norm, length).astype(BF16)


def middle_kernel(*refs):
    own, near, (high, low, proj_weight, texts_a, texts_b) = refs[:4], refs[4:8], refs[8:13]
    outs = refs[13:]
    for k, (unit, norm, length, grad) in enumerate((own, near)):
        slopes = slopes_of(unit[...], texts_b[...], False)
        outs[2 * k][...] = slopes
        total = grad[...] + jnp.dot(slopes, texts_b[...], preferred_element_type=F32)
        total = project(LOGIT_SCALE * total, norm[...], length[...])
        outs[2 * k + 1][...] = total.astype(BF16)
    block = whole_block(stacked((high, low)), proj_weight, texts_a, texts_b)
    for out, value in zip(outs[4:], block):
        out[...] = value


def late_kernel(*refs):
    core = lax.axis_index("c")
    feats, grads, (proj_weight, texts_a, texts_b) = refs[:7], refs[7:10], refs[10:13]
    unit_out, slopes_a, slopes_b, mine_out, other_out, weight = refs[13:]
    unit_out[...], slopes_a[...], slopes_b[...], far_grad = whole_block(
        stacked(feats[5:]), proj_weight, texts_a, texts_b
    )
    grads = jnp.concatenate([stacked(grads), far_grad])
    weight[...] = jnp.dot(stacked(feats).T, grads, preferred_element_type=F32)
    slices, rows = mine_out.shape[0], mine_out.shape[1]
    for k in range(slices):
        start = 2 * k * rows
        mine = pl.ds(pl.multiple_of(start + core * rows, rows), rows)
        other = pl.ds(pl.multiple_of(start + (1 - core) * rows, rows), rows)
        mine_out[k] = weight[mine]
        other_out[k] = weight[other].astype(BF16)


def add_kernel(mine, received, out):
    out[...] = (mine[...] + received[...].astype(F32)).astype(BF16)


def text_rows(units, slopes, start, stop):
    return LOGIT_SCALE * sum(
        jnp.dot(s[...].T[start:stop], u[...], preferred_element_type=F32)
        for s, u in zip(slopes, units)
    )


def text_kernel(count, *refs):
    units, slopes, (home, away) = refs[:count], refs[count : 2 * count], refs[2 * count :]
    rows = home.shape[0]
    total = text_rows(units, slopes, 0, 2 * rows)
    home[...], away[...] = total[:rows], total[rows:]


def away_kernel(count, *refs):
    units, slopes, away = refs[:count], refs[count : 2 * count], refs[2 * count]
    rows = away.shape[0]
    away[...] = text_rows(units, slopes, rows, 2 * rows)


def home_kernel(count, *refs):
    units, slopes, (received, feats, out) = refs[:count], refs[count : 2 * count], refs[2 * count :]
    total = received[...] + text_rows(units, slopes, 0, out.shape[0])
    out[...] = project(total, *normalize(feats[...].astype(F32))).astype(out.dtype)


def final_kernel(home, received, rest, feats, out):
    norm, length = normalize(feats[...].astype(F32))
    out[...] = project(home[...] + received[...], norm, length) + rest[...].astype(F32)


def call(kernel, outs, operands, mib, scratch=()):
    vmem = pl.BlockSpec(memory_space=pltpu.VMEM)
    shapes = tuple(jax.ShapeDtypeStruct(*out) for out in outs)
    return pl.pallas_call(
        kernel,
        out_shape=shapes,
        in_specs=[vmem] * len(operands),
        out_specs=(vmem,) * len(shapes),
        scratch_shapes=scratch,
        compiler_params=pltpu.CompilerParams(vmem_limit_bytes=mib * 1024 * 1024),
        cost_estimate=pl.CostEstimate(flops=1, bytes_accessed=1, transcendentals=0),
    )(*operands)


def local(sensor_feats, proj_weight, text_feats):
    rows, depth = sensor_feats.shape
    width = proj_weight.shape[1]
    half, texts = rows // 2, 2 * rows
    unit_like, grad_like = ((rows, width), BF16), ((rows, width), F32)
    slopes_like = ((rows, texts), BF16)

    text_c, text_y = send(text_feats, c=1), send(text_feats, yh=1)
    low, high = sensor_feats[:half], sensor_feats[half:]
    right_low, left_high = send(low, x=1), send(high, x=-1)
    right_high, left_low = send(high, x=1), send(low, x=-1)

    def units(first, second):
        return call(unit_kernel, [((texts, width), BF16)], [first, second], 12)[0]

    def early(feats, diagonal):
        return call(
            functools.partial(early_kernel, len(feats), diagonal),
            [unit_like, grad_like, ((rows, 1), F32), slopes_like, grad_like],
            [*feats, proj_weight, texts_a],
            16,
        )

    texts_a = units(text_feats, text_c)
    unit, norm, length, slopes_a, grad = early([sensor_feats], True)
    right_low, left_high, grad = lax.optimization_barrier((right_low, left_high, grad))
    far_low, far_high = send(right_low, x=1), send(left_high, x=-1)
    near_unit, near_norm, near_length, near_a, near = early([right_low, left_high], False)
    text_y, right_high, left_low, near = lax.optimization_barrier(
        (text_y, right_high, left_low, near)
    )
    texts_b = units(text_y, send(text_y, c=1))
    slopes_b, raw_grad, near_b, near_grad, next_unit, next_a, next_b, next_grad = call(
        middle_kernel,
        [
            slopes_like, unit_like, slopes_like, unit_like,
            unit_like, slopes_like, slopes_like, unit_like,
        ],
        [
            unit, norm, length, grad, near_unit, near_norm, near_length, near,
            right_high, left_low, proj_weight, texts_a, texts_b,
        ],
        30,
    )
    next_grad, far_low, far_high = lax.optimization_barrier((next_grad, far_low, far_high))
    share = (8, depth // 16, width)
    far_unit, far_a, far_b, mine, other = call(
        late_kernel,
        [unit_like, slopes_like, slopes_like, (share, F32), (share, BF16)],
        [
            sensor_feats, right_low, left_high, right_high, left_low,
            far_low, far_high, raw_grad, near_grad, next_grad, proj_weight, texts_a, texts_b,
        ],
        30,
        scratch=[pltpu.VMEM((depth, width), F32)],
    )

    def text_sums(kernel, outs, mib, slopes, *others):
        operands = [unit, near_unit, next_unit, far_unit, *slopes, *others]
        return call(functools.partial(kernel, 4), outs, operands, mib)

    weight_recv = send(other, c=1)
    half_b = [slopes_b, near_b, next_b, far_b]
    away_b = text_sums(away_kernel, [grad_like], 20, half_b)[0]
    weight_recv, away_b = lax.optimization_barrier((weight_recv, away_b))
    weight_sum = call(add_kernel, [(share, BF16)], [mine, weight_recv], 12)[0]
    weight_all = lax.all_to_all(weight_sum, ("x", "yh"), split_axis=0, concat_axis=0, tiled=True)
    text_send = text_sums(home_kernel, [unit_like], 58, half_b, send(away_b, c=1), text_y)[0]
    text_out = send(text_send, yh=1)
    slopes_a, text_send = lax.optimization_barrier((slopes_a, text_send))
    home_a, away_a = text_sums(text_kernel, [grad_like] * 2, 58, [slopes_a, near_a, next_a, far_a])
    away_a = send(away_a, c=1)

    weight_sum = jnp.sum(weight_all.astype(F32), axis=0).astype(BF16)
    across = send(weight_sum, z=2)
    ahead, behind = send(weight_sum, z=1), send(weight_sum, z=-1)
    weight_sum = (
        (weight_sum.astype(F32) + across.astype(F32)) + (ahead.astype(F32) + behind.astype(F32))
    ).astype(BF16)
    weight_sum, text_out = lax.optimization_barrier((weight_sum, text_out))
    across = send(weight_sum, yl=1)
    text_grad = call(final_kernel, [grad_like], [home_a, away_a, text_out, text_feats], 16)[0]
    across, text_grad = lax.optimization_barrier((across, text_grad))
    return (text_grad, weight_sum.astype(F32) + across.astype(F32))


def solution(mesh):
    fine = Mesh(mesh.devices.reshape(SIZES), AXES)
    return jax.shard_map(
        local,
        mesh=fine,
        in_specs=(P(AXES, None), P(), P(AXES, None)),
        out_specs=(P(AXES, None), P(("x", "yh", "c"), None)),
        check_vma=False,
    )
```

```python
import functools
import itertools

import jax
import jax.numpy as jnp
from jax import lax
from jax.experimental import pallas as pl
from jax.experimental.pallas import tpu as pltpu
from jax.sharding import Mesh, PartitionSpec as P

LOGIT_SCALE = 10.0
LOGIT_BIAS = -2.0
EPSILON = 1e-06

SIZES = (4, 2, 2, 4, 2)
AXES = ("x", "yh", "c", "z", "yl")
F32 = jnp.float32
BF16 = jnp.bfloat16


def position(coords):
    index = 0
    for size, coord in zip(SIZES, coords):
        index = index * size + coord % size
    return index


def send(block, **shift):
    step = [shift.get(name, 0) for name in AXES]
    route = [
        (position(at), position([a + s for a, s in zip(at, step)]))
        for at in itertools.product(*map(range, SIZES))
    ]
    return lax.ppermute(block, AXES, route)


def normalize(values):
    length = jnp.sqrt(jnp.sum(values * values, axis=-1, keepdims=True) + EPSILON)
    return (values / length, length)


def project(grad, norm, length):
    return (grad - norm * jnp.sum(norm * grad, axis=-1, keepdims=True)) / length


def slopes_of(unit, texts, diagonal):
    logits = LOGIT_SCALE * jnp.dot(unit, texts.T, preferred_element_type=F32) + LOGIT_BIAS
    slopes = jax.nn.sigmoid(logits)
    if diagonal:
        rows = lax.broadcasted_iota(jnp.int32, slopes.shape, 0)
        columns = lax.broadcasted_iota(jnp.int32, slopes.shape, 1)
        slopes = slopes - (rows == columns).astype(F32)
    return slopes.astype(BF16)


def text_units(first, second, out):
    rows = first.shape[0]
    out[:rows] = normalize(first[...].astype(F32))[0].astype(BF16)
    out[rows:] = normalize(second[...].astype(F32))[0].astype(BF16)


def stacked(refs):
    blocks = [ref[...] for ref in refs]
    return blocks[0] if len(blocks) == 1 else jnp.concatenate(blocks)


def first_kernel(feats, proj_weight, text, text_c, *outs):
    text_units(text, text_c, outs[0])
    early_kernel(1, True, feats, proj_weight, *outs)


def early_kernel(count, diagonal, *refs):
    feats, (proj_weight, texts) = refs[:count], refs[count : count + 2]
    unit_out, norm_out, length_out, slopes_out, grad_out = refs[count + 2 :]
    raw = jnp.dot(stacked(feats), proj_weight[...], preferred_element_type=F32)
    norm, length = normalize(raw)
    unit = norm.astype(BF16)
    unit_out[...], norm_out[...], length_out[...] = unit, norm, length
    slopes = slopes_of(unit, texts[...], diagonal)
    slopes_out[...] = slopes
    grad_out[...] = jnp.dot(slopes, texts[...], preferred_element_type=F32)


def whole_block(feats, proj_weight, texts_a, texts_b):
    raw = jnp.dot(feats, proj_weight[...], preferred_element_type=F32)
    norm, length = normalize(raw)
    unit = norm.astype(BF16)
    slopes_a = slopes_of(unit, texts_a[...], False)
    slopes_b = slopes_of(unit, texts_b[...], False)
    grad = jnp.dot(slopes_a, texts_a[...], preferred_element_type=F32)
    grad = grad + jnp.dot(slopes_b, texts_b[...], preferred_element_type=F32)
    return unit, slopes_a, slopes_b, project(LOGIT_SCALE * grad, norm, length).astype(BF16)


def middle_kernel(*refs):
    own, near, (high, low, proj_weight, texts_a) = refs[:4], refs[4:8], refs[8:12]
    (text_y, text_yc, texts_b), outs = refs[12:15], refs[15:]
    text_units(text_y, text_yc, texts_b)
    for k, (unit, norm, length, grad) in enumerate((own, near)):
        slopes = slopes_of(unit[...], texts_b[...], False)
        outs[2 * k][...] = slopes
        total = grad[...] + jnp.dot(slopes, texts_b[...], preferred_element_type=F32)
        total = project(LOGIT_SCALE * total, norm[...], length[...])
        outs[2 * k + 1][...] = total.astype(BF16)
    block = whole_block(stacked((high, low)), proj_weight, texts_a, texts_b)
    for out, value in zip(outs[4:], block):
        out[...] = value


def late_kernel(*refs):
    core = lax.axis_index("c")
    feats, grads, (proj_weight, texts_a, texts_b) = refs[:7], refs[7:10], refs[10:13]
    unit_out, slopes_a, slopes_b, mine_out, other_out, weight = refs[13:]
    unit_out[...], slopes_a[...], slopes_b[...], far_grad = whole_block(
        stacked(feats[5:]), proj_weight, texts_a, texts_b
    )
    grads = jnp.concatenate([stacked(grads), far_grad])
    weight[...] = jnp.dot(stacked(feats).T, grads, preferred_element_type=F32)
    slices, rows = mine_out.shape[0], mine_out.shape[1]
    for k in range(slices):
        start = 2 * k * rows
        mine = pl.ds(pl.multiple_of(start + core * rows, rows), rows)
        other = pl.ds(pl.multiple_of(start + (1 - core) * rows, rows), rows)
        mine_out[k] = weight[mine]
        other_out[k] = weight[other].astype(BF16)


def add_kernel(mine, received, out):
    out[...] = (mine[...] + received[...].astype(F32)).astype(BF16)


def text_rows(units, slopes, start, stop):
    return LOGIT_SCALE * sum(
        jnp.dot(s[...].T[start:stop], u[...], preferred_element_type=F32)
        for s, u in zip(slopes, units)
    )


def away_kernel(count, *refs):
    units, slopes, away = refs[:count], refs[count : 2 * count], refs[2 * count]
    rows = away.shape[0]
    away[...] = text_rows(units, slopes, rows, 2 * rows)


def home_kernel(count, *refs):
    units, slopes_a, slopes_b = (refs[k * count : (k + 1) * count] for k in range(3))
    received, feats, y_out, home, away = refs[3 * count :]
    rows = feats.shape[0]
    total = received[...] + text_rows(units, slopes_b, 0, rows)
    y_out[...] = project(total, *normalize(feats[...].astype(F32))).astype(BF16)
    total = text_rows(units, slopes_a, 0, 2 * rows)
    home[...], away[...] = total[:rows], total[rows:]


def final_kernel(home, received, rest, feats, out):
    norm, length = normalize(feats[...].astype(F32))
    out[...] = project(home[...] + received[...], norm, length) + rest[...].astype(F32)


def call(kernel, outs, operands, mib, scratch=()):
    vmem = pl.BlockSpec(memory_space=pltpu.VMEM)
    shapes = tuple(jax.ShapeDtypeStruct(*out) for out in outs)
    return pl.pallas_call(
        kernel,
        out_shape=shapes,
        in_specs=[vmem] * len(operands),
        out_specs=(vmem,) * len(shapes),
        scratch_shapes=scratch,
        compiler_params=pltpu.CompilerParams(vmem_limit_bytes=mib * 1024 * 1024),
        cost_estimate=pl.CostEstimate(flops=1, bytes_accessed=1, transcendentals=0),
    )(*operands)


def local(sensor_feats, proj_weight, text_feats):
    rows, depth = sensor_feats.shape
    width = proj_weight.shape[1]
    half, texts = rows // 2, 2 * rows
    unit_like, grad_like = ((rows, width), BF16), ((rows, width), F32)
    slopes_like = ((rows, texts), BF16)

    low, high, text = lax.optimization_barrier(
        (sensor_feats[:half], sensor_feats[half:], text_feats)
    )
    text_c, text_y = send(text, c=1), send(text, yh=1)
    right_low, left_high = send(low, x=1), send(high, x=-1)
    right_high, left_low = send(high, x=1), send(low, x=-1)

    texts_like = ((texts, width), BF16)
    early_like = [unit_like, grad_like, ((rows, 1), F32), slopes_like, grad_like]
    texts_a, unit, norm, length, slopes_a, grad = call(
        first_kernel, [texts_like, *early_like], [sensor_feats, proj_weight, text_feats, text_c], 18
    )
    right_low, left_high, grad = lax.optimization_barrier((right_low, left_high, grad))
    far_low, far_high = send(right_low, x=1), send(left_high, x=-1)
    near_unit, near_norm, near_length, near_a, near = call(
        functools.partial(early_kernel, 2, False),
        early_like, [right_low, left_high, proj_weight, texts_a], 16,
    )
    text_y, right_high, left_low, near = lax.optimization_barrier(
        (text_y, right_high, left_low, near)
    )
    texts_b, slopes_b, raw_grad, near_b, near_grad, next_unit, next_a, next_b, next_grad = call(
        middle_kernel,
        [
            texts_like, slopes_like, unit_like, slopes_like, unit_like,
            unit_like, slopes_like, slopes_like, unit_like,
        ],
        [
            unit, norm, length, grad, near_unit, near_norm, near_length, near,
            right_high, left_low, proj_weight, texts_a, text_y, send(text_y, c=1),
        ],
        30,
    )
    next_grad, far_low, far_high = lax.optimization_barrier((next_grad, far_low, far_high))
    share = (8, depth // 16, width)
    far_unit, far_a, far_b, mine, other = call(
        late_kernel,
        [unit_like, slopes_like, slopes_like, (share, F32), (share, BF16)],
        [
            sensor_feats, right_low, left_high, right_high, left_low,
            far_low, far_high, raw_grad, near_grad, next_grad, proj_weight, texts_a, texts_b,
        ],
        30,
        scratch=[pltpu.VMEM((depth, width), F32)],
    )

    def text_sums(kernel, outs, mib, slopes, *others):
        operands = [unit, near_unit, next_unit, far_unit, *slopes, *others]
        return call(functools.partial(kernel, 4), outs, operands, mib)

    weight_recv = send(other, c=1)
    half_b = [slopes_b, near_b, next_b, far_b]
    away_b = text_sums(away_kernel, [grad_like], 20, half_b)[0]
    weight_recv, away_b = lax.optimization_barrier((weight_recv, away_b))
    weight_sum = call(add_kernel, [(share, BF16)], [mine, weight_recv], 12)[0]
    weight_all = lax.all_to_all(weight_sum, ("x", "yh"), split_axis=0, concat_axis=0, tiled=True)
    text_send, home_a, away_a = text_sums(
        home_kernel,
        [unit_like, grad_like, grad_like],
        58,
        [slopes_a, near_a, next_a, far_a, *half_b],
        send(away_b, c=1),
        text_y,
    )
    text_out, away_a = send(text_send, yh=1), send(away_a, c=1)

    weight_sum = jnp.sum(weight_all.astype(F32), axis=0).astype(BF16)
    across = send(weight_sum, z=2)
    ahead, behind = send(weight_sum, z=1), send(weight_sum, z=-1)
    weight_sum = (
        (weight_sum.astype(F32) + across.astype(F32)) + (ahead.astype(F32) + behind.astype(F32))
    ).astype(BF16)
    across = send(weight_sum, yl=1)
    text_grad = call(final_kernel, [grad_like], [home_a, away_a, text_out, text_feats], 16)[0]
    across, text_grad = lax.optimization_barrier((across, text_grad))
    return (text_grad, weight_sum.astype(F32) + across.astype(F32))


def solution(mesh):
    fine = Mesh(mesh.devices.reshape(SIZES), AXES)
    return jax.shard_map(
        local,
        mesh=fine,
        in_specs=(P(AXES, None), P(), P(AXES, None)),
        out_specs=(P(AXES, None), P(("x", "yh", "c"), None)),
        check_vma=False,
    )
```

```python
import functools
import itertools

import jax
import jax.numpy as jnp
from jax import lax
from jax.experimental import pallas as pl
from jax.experimental.pallas import tpu as pltpu
from jax.sharding import Mesh, PartitionSpec as P

LOGIT_SCALE = 10.0
LOGIT_BIAS = -2.0
EPSILON = 1e-06

SIZES = (4, 2, 2, 4, 2)
AXES = ("x", "yh", "c", "z", "yl")
F32 = jnp.float32
BF16 = jnp.bfloat16


def position(coords):
    index = 0
    for size, coord in zip(SIZES, coords):
        index = index * size + coord % size
    return index


def send(block, **shift):
    step = [shift.get(name, 0) for name in AXES]
    route = [
        (position(at), position([a + s for a, s in zip(at, step)]))
        for at in itertools.product(*map(range, SIZES))
    ]
    return lax.ppermute(block, AXES, route)


def normalize(values):
    length = jnp.sqrt(jnp.sum(values * values, axis=-1, keepdims=True) + EPSILON)
    return (values / length, length)


def project(grad, norm, length):
    return (grad - norm * jnp.sum(norm * grad, axis=-1, keepdims=True)) / length


def slopes_of(unit, texts, diagonal):
    logits = LOGIT_SCALE * jnp.dot(unit, texts.T, preferred_element_type=F32) + LOGIT_BIAS
    slopes = jax.nn.sigmoid(logits)
    if diagonal:
        rows = lax.broadcasted_iota(jnp.int32, slopes.shape, 0)
        columns = lax.broadcasted_iota(jnp.int32, slopes.shape, 1)
        slopes = slopes - (rows == columns).astype(F32)
    return slopes.astype(BF16)


def text_units(first, second, out):
    rows = first.shape[0]
    out[:rows] = normalize(first.astype(F32))[0].astype(BF16)
    out[rows:] = normalize(second.astype(F32))[0].astype(BF16)


def stacked(refs):
    blocks = [ref[...] for ref in refs]
    return blocks[0] if len(blocks) == 1 else jnp.concatenate(blocks)


def first_kernel(feats, proj_weight, text, text_c, *outs):
    text_units(text[...], text_c[...], outs[0])
    early_kernel(1, True, feats, proj_weight, *outs)


def early_kernel(count, diagonal, *refs):
    feats, (proj_weight, texts) = refs[:count], refs[count : count + 2]
    unit_out, norm_out, length_out, slopes_out, grad_out = refs[count + 2 :]
    raw = jnp.dot(stacked(feats), proj_weight[...], preferred_element_type=F32)
    norm, length = normalize(raw)
    unit = norm.astype(BF16)
    unit_out[...], norm_out[...], length_out[...] = unit, norm, length
    slopes = slopes_of(unit, texts[...], diagonal)
    slopes_out[...] = slopes
    grad_out[...] = jnp.dot(slopes, texts[...], preferred_element_type=F32)


def whole_block(feats, proj_weight, texts_a, texts_b):
    raw = jnp.dot(feats, proj_weight[...], preferred_element_type=F32)
    norm, length = normalize(raw)
    unit = norm.astype(BF16)
    slopes_a = slopes_of(unit, texts_a[...], False)
    slopes_b = slopes_of(unit, texts_b[...], False)
    grad = jnp.dot(slopes_a, texts_a[...], preferred_element_type=F32)
    grad = grad + jnp.dot(slopes_b, texts_b[...], preferred_element_type=F32)
    return unit, slopes_a, slopes_b, project(LOGIT_SCALE * grad, norm, length).astype(BF16)


def middle_kernel(count, *refs):
    early, (text_y, *text_yc), (texts, *outs) = (
        refs[: 4 * count], refs[4 * count : 4 * count + 3], refs[4 * count + 3 :]
    )
    text_units(text_y[...], stacked(text_yc), texts)
    for k in range(count):
        unit, norm, length, grad = early[4 * k : 4 * k + 4]
        slopes = slopes_of(unit[...], texts[...], False)
        outs[2 * k][...] = slopes
        total = grad[...] + jnp.dot(slopes, texts[...], preferred_element_type=F32)
        total = project(LOGIT_SCALE * total, norm[...], length[...])
        outs[2 * k + 1][...] = total.astype(BF16)


def late_kernel(*refs):
    core = lax.axis_index("c")
    feats, (low, high), grads = refs[:5], refs[5:7], refs[7:10]
    (proj_weight, texts_a, texts_b), outs = refs[10:13], refs[13:]
    unit_out, slopes_a, slopes_b, mine_out, other_out, weight = outs
    half = unit_out.shape[0] // 2
    far = jnp.concatenate([low[:half], high[high.shape[0] - half :]])
    unit_out[...], slopes_a[...], slopes_b[...], far_grad = whole_block(
        far, proj_weight, texts_a, texts_b
    )
    feats = jnp.concatenate([stacked(feats), far])
    grads = jnp.concatenate([stacked(grads), far_grad])
    weight[...] = jnp.dot(feats.T, grads, preferred_element_type=F32)
    slices, rows = mine_out.shape[0], mine_out.shape[1]
    for k in range(slices):
        start = 2 * k * rows
        mine = pl.ds(pl.multiple_of(start + core * rows, rows), rows)
        other = pl.ds(pl.multiple_of(start + (1 - core) * rows, rows), rows)
        mine_out[k] = weight[mine]
        other_out[k] = weight[other].astype(BF16)


def add_kernel(mine, received, out):
    out[...] = (mine[...] + received[...].astype(F32)).astype(BF16)


def text_rows(units, slopes, start, stop):
    return LOGIT_SCALE * sum(
        jnp.dot(s[...].T[start:stop], u[...], preferred_element_type=F32)
        for s, u in zip(slopes, units)
    )


def away_kernel(count, *refs):
    units, slopes, away = refs[:count], refs[count : 2 * count], refs[2 * count]
    rows = away.shape[0]
    away[...] = text_rows(units, slopes, rows, 2 * rows)


def home_kernel(count, *refs):
    units, slopes_a, slopes_b = (refs[k * count : (k + 1) * count] for k in range(3))
    received, feats, y_out, home, away = refs[3 * count :]
    rows = feats.shape[0]
    total = received[...] + text_rows(units, slopes_b, 0, rows)
    y_out[...] = project(total, *normalize(feats[...].astype(F32))).astype(BF16)
    total = text_rows(units, slopes_a, 0, 2 * rows)
    home[...], away[...] = total[:rows], total[rows:]


def final_kernel(home, received, rest, feats, out):
    norm, length = normalize(feats[...].astype(F32))
    out[...] = project(home[...] + received[...], norm, length) + rest[...].astype(F32)


def call(kernel, outs, operands, mib, scratch=()):
    vmem = pl.BlockSpec(memory_space=pltpu.VMEM)
    shapes = tuple(jax.ShapeDtypeStruct(*out) for out in outs)
    return pl.pallas_call(
        kernel,
        out_shape=shapes,
        in_specs=[vmem] * len(operands),
        out_specs=(vmem,) * len(shapes),
        scratch_shapes=scratch,
        compiler_params=pltpu.CompilerParams(vmem_limit_bytes=mib * 1024 * 1024),
        cost_estimate=pl.CostEstimate(flops=1, bytes_accessed=1, transcendentals=0),
    )(*operands)


def local(sensor_feats, proj_weight, text_feats):
    rows, depth = sensor_feats.shape
    width = proj_weight.shape[1]
    half, texts = rows // 2, 2 * rows
    more, less = half + 16, half - 16

    def early_like(rows):
        return [
            ((rows, width), BF16), ((rows, width), F32), ((rows, 1), F32),
            ((rows, texts), BF16), ((rows, width), F32),
        ]

    def early(*feats):
        return call(
            functools.partial(early_kernel, 2, False),
            early_like(sum(f.shape[0] for f in feats)), [*feats, proj_weight, texts_a], 18,
        )

    low, high, text = lax.optimization_barrier(
        (sensor_feats[:more], sensor_feats[less:], text_feats)
    )
    text_c, text_y = send(text, c=1), send(text, yh=1)
    right_low, left_high = send(low, x=1), send(high, x=-1)
    right_rest = send(sensor_feats[more:], x=1)
    left_rest = send(sensor_feats[:less], x=-1)

    texts_like = ((texts, width), BF16)
    unit_like, grad_like, _, slopes_like, _ = early_like(rows)
    texts_a, unit, norm, length, slopes_a, grad = call(
        first_kernel,
        [texts_like, *early_like(rows)], [sensor_feats, proj_weight, text_feats, text_c], 18,
    )
    right_low, left_high, grad = lax.optimization_barrier((right_low, left_high, grad))
    far_low, far_high = send(right_low, x=1), send(left_high, x=-1)
    near_unit, near_norm, near_length, near_a, near = early(right_low, left_high)
    text_y, right_rest, left_rest, near = lax.optimization_barrier(
        (text_y, right_rest, left_rest, near)
    )
    text_yc = [send(text_y[:half], c=1), send(text_y[half:], c=1)]
    next_unit, next_norm, next_length, next_a, next_ = early(right_rest, left_rest)
    groups = [
        (unit, norm, length, grad),
        (near_unit, near_norm, near_length, near),
        (next_unit, next_norm, next_length, next_),
    ]
    outs = [[((g[0].shape[0], texts), BF16), ((g[0].shape[0], width), BF16)] for g in groups]
    texts_b, slopes_b, raw_grad, near_b, near_grad, next_b, next_grad = call(
        functools.partial(middle_kernel, 3),
        [texts_like, *itertools.chain(*outs)],
        [*itertools.chain(*groups), text_y, *text_yc],
        32,
    )
    next_grad, far_low, far_high = lax.optimization_barrier((next_grad, far_low, far_high))
    share = (8, depth // 16, width)
    far_unit, far_a, far_b, mine, other = call(
        late_kernel,
        [unit_like, slopes_like, slopes_like, (share, F32), (share, BF16)],
        [
            sensor_feats, right_low, left_high, right_rest, left_rest, far_low, far_high,
            raw_grad, near_grad, next_grad, proj_weight, texts_a, texts_b,
        ],
        30,
        scratch=[pltpu.VMEM((depth, width), F32)],
    )

    def text_sums(kernel, outs, mib, slopes, *others):
        operands = [unit, near_unit, next_unit, far_unit, *slopes, *others]
        return call(functools.partial(kernel, 4), outs, operands, mib)

    weight_recv = send(other, c=1)
    half_b = [slopes_b, near_b, next_b, far_b]
    away_b = text_sums(away_kernel, [grad_like], 20, half_b)[0]
    weight_recv, away_b = lax.optimization_barrier((weight_recv, away_b))
    weight_sum = call(add_kernel, [(share, BF16)], [mine, weight_recv], 12)[0]
    weight_all = lax.all_to_all(weight_sum, ("x", "yh"), split_axis=0, concat_axis=0, tiled=True)
    text_send, home_a, away_a = text_sums(
        home_kernel,
        [unit_like, grad_like, grad_like],
        58,
        [slopes_a, near_a, next_a, far_a, *half_b],
        send(away_b, c=1),
        text_y,
    )
    text_out, away_a = send(text_send, yh=1), send(away_a, c=1)

    weight_sum = jnp.sum(weight_all.astype(F32), axis=0).astype(BF16)
    across = send(weight_sum, z=2)
    ahead, behind = send(weight_sum, z=1), send(weight_sum, z=-1)
    weight_sum = (
        (weight_sum.astype(F32) + across.astype(F32)) + (ahead.astype(F32) + behind.astype(F32))
    ).astype(BF16)
    across = send(weight_sum, yl=1)
    text_grad = call(final_kernel, [grad_like], [home_a, away_a, text_out, text_feats], 16)[0]
    across, text_grad = lax.optimization_barrier((across, text_grad))
    return (text_grad, weight_sum.astype(F32) + across.astype(F32))


def solution(mesh):
    fine = Mesh(mesh.devices.reshape(SIZES), AXES)
    return jax.shard_map(
        local,
        mesh=fine,
        in_specs=(P(AXES, None), P(), P(AXES, None)),
        out_specs=(P(AXES, None), P(("x", "yh", "c"), None)),
        check_vma=False,
    )
```

```python
import functools
import itertools

import jax
import jax.numpy as jnp
from jax import lax
from jax.experimental import pallas as pl
from jax.experimental.pallas import tpu as pltpu
from jax.sharding import Mesh, PartitionSpec as P

LOGIT_SCALE = 10.0
LOGIT_BIAS = -2.0
EPSILON = 1e-06

SIZES = (4, 2, 2, 4, 2)
AXES = ("x", "yh", "c", "z", "yl")
F32 = jnp.float32
BF16 = jnp.bfloat16


def position(coords):
    index = 0
    for size, coord in zip(SIZES, coords):
        index = index * size + coord % size
    return index


def send(block, **shift):
    step = [shift.get(name, 0) for name in AXES]
    route = [
        (position(at), position([a + s for a, s in zip(at, step)]))
        for at in itertools.product(*map(range, SIZES))
    ]
    return lax.ppermute(block, AXES, route)


def normalize(values):
    length = jnp.sqrt(jnp.sum(values * values, axis=-1, keepdims=True) + EPSILON)
    return (values / length, length)


def project(grad, norm, length):
    return (grad - norm * jnp.sum(norm * grad, axis=-1, keepdims=True)) / length


def slopes_of(unit, texts, diagonal):
    logits = LOGIT_SCALE * jnp.dot(unit, texts.T, preferred_element_type=F32) + LOGIT_BIAS
    slopes = jax.nn.sigmoid(logits)
    if diagonal:
        rows = lax.broadcasted_iota(jnp.int32, slopes.shape, 0)
        columns = lax.broadcasted_iota(jnp.int32, slopes.shape, 1)
        slopes = slopes - (rows == columns).astype(F32)
    return slopes.astype(BF16)


def unit_rows(texts):
    return normalize(texts.astype(F32))[0].astype(BF16)


def stacked(refs):
    blocks = [ref[...] for ref in refs]
    return blocks[0] if len(blocks) == 1 else jnp.concatenate(blocks)


def first_kernel(feats, proj_weight, text, text_c, rest, *outs):
    texts, rows = outs[0], text.shape[0]
    units = unit_rows(text_c[...])
    texts[:rows], texts[rows:] = unit_rows(text[...]), units[: texts.shape[0] - rows]
    rest[...] = units[texts.shape[0] - rows :]
    early_kernel(1, True, feats, proj_weight, *outs)


def early_kernel(count, diagonal, *refs):
    feats, (proj_weight, texts) = refs[:count], refs[count : count + 2]
    unit_out, norm_out, length_out, slopes_out, grad_out = refs[count + 2 :]
    raw = jnp.dot(stacked(feats), proj_weight[...], preferred_element_type=F32)
    norm, length = normalize(raw)
    unit = norm.astype(BF16)
    unit_out[...], norm_out[...], length_out[...] = unit, norm, length
    slopes = slopes_of(unit, texts[...], diagonal)
    slopes_out[...] = slopes
    grad_out[...] = jnp.dot(slopes, texts[...], preferred_element_type=F32)


def whole_block(feats, proj_weight, texts_a, texts_b):
    raw = jnp.dot(feats, proj_weight[...], preferred_element_type=F32)
    norm, length = normalize(raw)
    unit = norm.astype(BF16)
    slopes_a = slopes_of(unit, texts_a[...], False)
    slopes_b = slopes_of(unit, texts_b[...], False)
    grad = jnp.dot(slopes_a, texts_a[...], preferred_element_type=F32)
    grad = grad + jnp.dot(slopes_b, texts_b[...], preferred_element_type=F32)
    return unit, slopes_a, slopes_b, project(LOGIT_SCALE * grad, norm, length).astype(BF16)


def middle_kernel(count, *refs):
    early, (rest, text_y, *text_yc), (texts, *outs) = (
        refs[: 4 * count], refs[4 * count : 4 * count + 4], refs[4 * count + 4 :]
    )
    rows = rest.shape[0]
    texts[:rows] = rest[...]
    texts[rows : rows + text_y.shape[0]] = unit_rows(text_y[...])
    texts[rows + text_y.shape[0] :] = unit_rows(stacked(text_yc))
    for k in range(count):
        unit, norm, length, grad = early[4 * k : 4 * k + 4]
        slopes = slopes_of(unit[...], texts[...], False)
        outs[2 * k][...] = slopes
        total = grad[...] + jnp.dot(slopes, texts[...], preferred_element_type=F32)
        total = project(LOGIT_SCALE * total, norm[...], length[...])
        outs[2 * k + 1][...] = total.astype(BF16)


def late_kernel(*refs):
    core = lax.axis_index("c")
    feats, (low, high), grads = refs[:5], refs[5:7], refs[7:10]
    (proj_weight, texts_a, texts_b), outs = refs[10:13], refs[13:]
    unit_out, slopes_a, slopes_b, mine_out, other_out, weight = outs
    half = unit_out.shape[0] // 2
    far = jnp.concatenate([low[:half], high[high.shape[0] - half :]])
    unit_out[...], slopes_a[...], slopes_b[...], far_grad = whole_block(
        far, proj_weight, texts_a, texts_b
    )
    feats = jnp.concatenate([stacked(feats), far])
    grads = jnp.concatenate([stacked(grads), far_grad])
    weight[...] = jnp.dot(feats.T, grads, preferred_element_type=F32)
    slices, rows = mine_out.shape[0], mine_out.shape[1]
    for k in range(slices):
        start = 2 * k * rows
        mine = pl.ds(pl.multiple_of(start + core * rows, rows), rows)
        other = pl.ds(pl.multiple_of(start + (1 - core) * rows, rows), rows)
        mine_out[k] = weight[mine]
        other_out[k] = weight[other].astype(BF16)


def add_kernel(mine, received, out):
    out[...] = (mine[...] + received[...].astype(F32)).astype(BF16)


def text_rows(units, slopes, start, stop):
    return LOGIT_SCALE * sum(
        jnp.dot(s[...].T[start:stop], u[...], preferred_element_type=F32)
        for s, u in zip(slopes, units)
    )


def away_kernel(count, *refs):
    units, slopes, away = refs[:count], refs[count : 2 * count], refs[2 * count]
    stop = slopes[0].shape[1]
    away[...] = text_rows(units, slopes, stop - away.shape[0], stop)


def home_kernel(count, *refs):
    units, slopes_a, slopes_b = (refs[k * count : (k + 1) * count] for k in range(3))
    received, feats_y, feats, feats_c, y_out, home, away = refs[3 * count :]
    rows, first = feats.shape[0], slopes_a[0].shape[1]
    rest = 2 * rows - first

    def through(total, feats):
        return project(total, *normalize(feats[...].astype(F32)))

    total = received[...] + text_rows(units, slopes_b, rest, rest + rows)
    y_out[...] = through(total, feats_y).astype(BF16)
    total = text_rows(units, slopes_a, 0, first)
    home[...] = through(total[:rows], feats)
    total = jnp.concatenate([total[rows:], text_rows(units, slopes_b, 0, rest)])
    away[...] = through(total, feats_c).astype(BF16)


def sum_kernel(parts, out):
    out[...] = jnp.sum(parts[...].astype(F32), axis=0).astype(out.dtype)


def add_text_kernel(first, second, out):
    out[...] = first[...] + second[...].astype(F32)


def call(kernel, outs, operands, mib, scratch=()):
    vmem = pl.BlockSpec(memory_space=pltpu.VMEM)
    shapes = tuple(jax.ShapeDtypeStruct(*out) for out in outs)
    return pl.pallas_call(
        kernel,
        out_shape=shapes,
        in_specs=[vmem] * len(operands),
        out_specs=(vmem,) * len(shapes),
        scratch_shapes=scratch,
        compiler_params=pltpu.CompilerParams(vmem_limit_bytes=mib * 1024 * 1024),
        cost_estimate=pl.CostEstimate(flops=1, bytes_accessed=1, transcendentals=0),
    )(*operands)


def local(sensor_feats, proj_weight, text_feats):
    rows, depth = sensor_feats.shape
    width = proj_weight.shape[1]
    half = rows // 2
    texts = 2 * rows // 256 * 256
    texts_rest = 4 * rows - texts
    more, less = half + 16, half - 16

    def early_like(rows):
        return [
            ((rows, width), BF16), ((rows, width), F32), ((rows, 1), F32),
            ((rows, texts), BF16), ((rows, width), F32),
        ]

    def early(*feats):
        return call(
            functools.partial(early_kernel, 2, False),
            early_like(sum(f.shape[0] for f in feats)), [*feats, proj_weight, texts_a], 18,
        )

    low, high, text = lax.optimization_barrier(
        (sensor_feats[:more], sensor_feats[less:], text_feats)
    )
    text_c, text_y = send(text, c=1), send(text, yh=1)
    right_low, left_high = send(low, x=1), send(high, x=-1)
    right_rest = send(sensor_feats[more:], x=1)
    left_rest = send(sensor_feats[:less], x=-1)

    texts_like, rest_like = ((texts, width), BF16), ((2 * rows - texts, width), BF16)
    unit_like, grad_like, _, slopes_like, _ = early_like(rows)
    rest, texts_a, unit, norm, length, slopes_a, grad = call(
        first_kernel,
        [rest_like, texts_like, *early_like(rows)], [sensor_feats, proj_weight, text_feats, text_c], 18,
    )
    right_low, left_high, grad = lax.optimization_barrier((right_low, left_high, grad))
    far_low, far_high = send(right_low, x=1), send(left_high, x=-1)
    near_unit, near_norm, near_length, near_a, near = early(right_low, left_high)
    text_y, right_rest, left_rest, near = lax.optimization_barrier(
        (text_y, right_rest, left_rest, near)
    )
    text_yc = [send(text_y[:half], c=1), send(text_y[half:], c=1)]
    next_unit, next_norm, next_length, next_a, next_ = early(right_rest, left_rest)
    groups = [
        (unit, norm, length, grad),
        (near_unit, near_norm, near_length, near),
        (next_unit, next_norm, next_length, next_),
    ]
    outs = [[((g[0].shape[0], texts_rest), BF16), ((g[0].shape[0], width), BF16)] for g in groups]
    texts_b, slopes_b, raw_grad, near_b, near_grad, next_b, next_grad = call(
        functools.partial(middle_kernel, 3),
        [((texts_rest, width), BF16), *itertools.chain(*outs)],
        [*itertools.chain(*groups), rest, text_y, *text_yc],
        24,
    )
    next_grad, far_low, far_high = lax.optimization_barrier((next_grad, far_low, far_high))
    share = (8, depth // 16, width)
    far_unit, far_a, far_b, mine, other = call(
        late_kernel,
        [unit_like, slopes_like, ((rows, texts_rest), BF16), (share, F32), (share, BF16)],
        [
            sensor_feats, right_low, left_high, right_rest, left_rest, far_low, far_high,
            raw_grad, near_grad, next_grad, proj_weight, texts_a, texts_b,
        ],
        24,
        scratch=[pltpu.VMEM((depth, width), F32)],
    )

    def text_sums(kernel, outs, mib, slopes, *others):
        operands = [unit, near_unit, next_unit, far_unit, *slopes, *others]
        return call(functools.partial(kernel, 4), outs, operands, mib)

    weight_recv = send(other, c=1)
    half_b = [slopes_b, near_b, next_b, far_b]
    away_b = text_sums(away_kernel, [grad_like], 20, half_b)[0]
    weight_recv, away_b = lax.optimization_barrier((weight_recv, away_b))
    weight_sum = call(add_kernel, [(share, BF16)], [mine, weight_recv], 12)[0]
    weight_all = lax.all_to_all(weight_sum, ("x", "yh"), split_axis=0, concat_axis=0, tiled=True)
    text_send, home_a, away_a = text_sums(
        home_kernel,
        [unit_like, grad_like, unit_like],
        58,
        [slopes_a, near_a, next_a, far_a, *half_b],
        send(away_b, c=1),
        text_y,
        text_feats,
        text_c,
    )
    text_out, away_a = send(text_send, yh=1), send(away_a, c=1)

    weight_sum = call(sum_kernel, [(share[1:], BF16)], [weight_all], 8)[0]
    across = send(weight_sum, z=2)
    ahead, behind = send(weight_sum, z=1), send(weight_sum, z=-1)
    home_a = call(add_text_kernel, [grad_like], [home_a, away_a], 12)[0]
    across, ahead, behind, home_a = lax.optimization_barrier((across, ahead, behind, home_a))
    weight_sum = (
        (weight_sum.astype(F32) + across.astype(F32)) + (ahead.astype(F32) + behind.astype(F32))
    ).astype(BF16)
    across = send(weight_sum, yl=1)
    text_grad = call(add_text_kernel, [grad_like], [home_a, text_out], 12)[0]
    across, text_grad = lax.optimization_barrier((across, text_grad))
    return (text_grad, weight_sum.astype(F32) + across.astype(F32))


def solution(mesh):
    fine = Mesh(mesh.devices.reshape(SIZES), AXES)
    return jax.shard_map(
        local,
        mesh=fine,
        in_specs=(P(AXES, None), P(), P(AXES, None)),
        out_specs=(P(AXES, None), P(("x", "yh", "c"), None)),
        check_vma=False,
    )
```

```python
import functools
import itertools

import jax
import jax.numpy as jnp
from jax import lax
from jax.experimental import pallas as pl
from jax.experimental.pallas import tpu as pltpu
from jax.sharding import Mesh, PartitionSpec as P

LOGIT_SCALE = 10.0
LOGIT_BIAS = -2.0
EPSILON = 1e-06

SIZES = (4, 2, 2, 4, 2)
AXES = ("x", "yh", "c", "z", "yl")
F32 = jnp.float32
BF16 = jnp.bfloat16


def position(coords):
    index = 0
    for size, coord in zip(SIZES, coords):
        index = index * size + coord % size
    return index


def send(block, **shift):
    step = [shift.get(name, 0) for name in AXES]
    route = [
        (position(at), position([a + s for a, s in zip(at, step)]))
        for at in itertools.product(*map(range, SIZES))
    ]
    return lax.ppermute(block, AXES, route)


def normalize(values):
    length = jnp.sqrt(jnp.sum(values * values, axis=-1, keepdims=True) + EPSILON)
    return (values / length, length)


def project(grad, norm, length):
    return (grad - norm * jnp.sum(norm * grad, axis=-1, keepdims=True)) / length


def slopes_of(unit, texts, diagonal):
    logits = LOGIT_SCALE * jnp.dot(unit, texts.T, preferred_element_type=F32) + LOGIT_BIAS
    slopes = jax.nn.sigmoid(logits)
    if diagonal:
        rows = lax.broadcasted_iota(jnp.int32, slopes.shape, 0)
        columns = lax.broadcasted_iota(jnp.int32, slopes.shape, 1)
        slopes = slopes - (rows == columns).astype(F32)
    return slopes.astype(BF16)


def unit_rows(texts):
    return normalize(texts.astype(F32))[0].astype(BF16)


def stacked(refs):
    blocks = [ref[...] for ref in refs]
    return blocks[0] if len(blocks) == 1 else jnp.concatenate(blocks)


def first_kernel(feats, proj_weight, text, text_c, rest, *outs):
    texts, rows = outs[0], text.shape[0]
    units = unit_rows(text_c[...])
    texts[:rows], texts[rows:] = unit_rows(text[...]), units[: texts.shape[0] - rows]
    rest[...] = units[texts.shape[0] - rows :]
    early_kernel(1, True, feats, proj_weight, *outs)


def early_kernel(count, diagonal, *refs):
    feats, (proj_weight, texts) = refs[:count], refs[count : count + 2]
    unit_out, norm_out, length_out, slopes_out, grad_out = refs[count + 2 :]
    raw = jnp.dot(stacked(feats), proj_weight[...], preferred_element_type=F32)
    norm, length = normalize(raw)
    unit = norm.astype(BF16)
    unit_out[...], norm_out[...], length_out[...] = unit, norm, length
    slopes = slopes_of(unit, texts[...], diagonal)
    slopes_out[...] = slopes
    grad_out[...] = jnp.dot(slopes, texts[...], preferred_element_type=F32)


def whole_block(feats, proj_weight, texts_a, texts_b):
    raw = jnp.dot(feats, proj_weight[...], preferred_element_type=F32)
    norm, length = normalize(raw)
    unit = norm.astype(BF16)
    slopes_a = slopes_of(unit, texts_a[...], False)
    slopes_b = slopes_of(unit, texts_b[...], False)
    grad = jnp.dot(slopes_a, texts_a[...], preferred_element_type=F32)
    grad = grad + jnp.dot(slopes_b, texts_b[...], preferred_element_type=F32)
    return unit, slopes_a, slopes_b, project(LOGIT_SCALE * grad, norm, length).astype(BF16)


def middle_kernel(count, *refs):
    early, (rest, text_y, *text_yc), (texts, *outs) = (
        refs[: 4 * count], refs[4 * count : 4 * count + 4], refs[4 * count + 4 :]
    )
    rows = rest.shape[0]
    texts[:rows] = rest[...]
    texts[rows : rows + text_y.shape[0]] = unit_rows(text_y[...])
    texts[rows + text_y.shape[0] :] = unit_rows(stacked(text_yc))
    for k in range(count):
        unit, norm, length, grad = early[4 * k : 4 * k + 4]
        slopes = slopes_of(unit[...], texts[...], False)
        outs[2 * k][...] = slopes
        total = grad[...] + jnp.dot(slopes, texts[...], preferred_element_type=F32)
        total = project(LOGIT_SCALE * total, norm[...], length[...])
        outs[2 * k + 1][...] = total.astype(BF16)


def late_kernel(*refs):
    core = lax.axis_index("c")
    feats, (low, high), grads = refs[:5], refs[5:7], refs[7:10]
    (proj_weight, texts_a, texts_b), outs = refs[10:13], refs[13:]
    unit_out, slopes_a, slopes_b, mine_out, other_out, flipped = outs
    half = unit_out.shape[0] // 2
    far = jnp.concatenate([low[:half], high[high.shape[0] - half :]])
    flipped[...] = jnp.concatenate([stacked(feats), far]).T
    unit_out[...], slopes_a[...], slopes_b[...], far_grad = whole_block(
        far, proj_weight, texts_a, texts_b
    )
    grads = jnp.concatenate([stacked(grads), far_grad])
    slices, rows, width = mine_out.shape
    for out, side in ((other_out, 1 - core), (mine_out, core)):
        starts = [pl.multiple_of((2 * k + side) * rows, rows) for k in range(slices)]
        part = jnp.concatenate([flipped[pl.ds(start, rows)] for start in starts])
        product = jnp.dot(part, grads, preferred_element_type=F32)
        out[...] = product.reshape(slices, rows, width).astype(out.dtype)


def add_kernel(mine, received, out):
    out[...] = (mine[...] + received[...].astype(F32)).astype(BF16)


def text_rows(units, slopes, start, stop):
    return LOGIT_SCALE * sum(
        jnp.dot(s[...].T[start:stop], u[...], preferred_element_type=F32)
        for s, u in zip(slopes, units)
    )


def away_kernel(count, *refs):
    units, slopes, away = refs[:count], refs[count : 2 * count], refs[2 * count]
    stop = slopes[0].shape[1]
    away[...] = text_rows(units, slopes, stop - away.shape[0], stop)


def home_kernel(count, *refs):
    units, slopes_a, slopes_b = (refs[k * count : (k + 1) * count] for k in range(3))
    received, feats_y, feats, feats_c, y_out, home, away = refs[3 * count :]
    rows, first = feats.shape[0], slopes_a[0].shape[1]
    rest = 2 * rows - first

    def through(total, feats):
        return project(total, *normalize(feats[...].astype(F32)))

    total = received[...] + text_rows(units, slopes_b, rest, rest + rows)
    y_out[...] = through(total, feats_y).astype(BF16)
    total = text_rows(units, slopes_a, 0, first)
    home[...] = through(total[:rows], feats)
    total = jnp.concatenate([total[rows:], text_rows(units, slopes_b, 0, rest)])
    away[...] = through(total, feats_c).astype(BF16)


def sum_kernel(parts, out):
    out[...] = jnp.sum(parts[...].astype(F32), axis=0).astype(out.dtype)


def add_text_kernel(first, second, out):
    out[...] = first[...] + second[...].astype(F32)


def call(kernel, outs, operands, mib, scratch=()):
    vmem = pl.BlockSpec(memory_space=pltpu.VMEM)
    shapes = tuple(jax.ShapeDtypeStruct(*out) for out in outs)
    return pl.pallas_call(
        kernel,
        out_shape=shapes,
        in_specs=[vmem] * len(operands),
        out_specs=(vmem,) * len(shapes),
        scratch_shapes=scratch,
        compiler_params=pltpu.CompilerParams(vmem_limit_bytes=mib * 1024 * 1024),
        cost_estimate=pl.CostEstimate(flops=1, bytes_accessed=1, transcendentals=0),
    )(*operands)


def local(sensor_feats, proj_weight, text_feats):
    rows, depth = sensor_feats.shape
    width = proj_weight.shape[1]
    half = rows // 2
    texts = 2 * rows // 256 * 256
    texts_rest = 4 * rows - texts
    more, less = half + 16, half - 16

    def early_like(rows):
        return [
            ((rows, width), BF16), ((rows, width), F32), ((rows, 1), F32),
            ((rows, texts), BF16), ((rows, width), F32),
        ]

    def early(*feats):
        return call(
            functools.partial(early_kernel, 2, False),
            early_like(sum(f.shape[0] for f in feats)), [*feats, proj_weight, texts_a], 18,
        )

    low, high, text = lax.optimization_barrier(
        (sensor_feats[:more], sensor_feats[less:], text_feats)
    )
    text_c, text_y = send(text, c=1), send(text, yh=1)
    right_low, left_high = send(low, x=1), send(high, x=-1)
    right_rest = send(sensor_feats[more:], x=1)
    left_rest = send(sensor_feats[:less], x=-1)

    texts_like, rest_like = ((texts, width), BF16), ((2 * rows - texts, width), BF16)
    unit_like, grad_like, _, slopes_like, _ = early_like(rows)
    rest, texts_a, unit, norm, length, slopes_a, grad = call(
        first_kernel,
        [rest_like, texts_like, *early_like(rows)], [sensor_feats, proj_weight, text_feats, text_c], 18,
    )
    right_low, left_high, grad = lax.optimization_barrier((right_low, left_high, grad))
    far_low, far_high = send(right_low, x=1), send(left_high, x=-1)
    near_unit, near_norm, near_length, near_a, near = early(right_low, left_high)
    text_y, right_rest, left_rest, near = lax.optimization_barrier(
        (text_y, right_rest, left_rest, near)
    )
    text_yc = [send(text_y[:half], c=1), send(text_y[half:], c=1)]
    next_unit, next_norm, next_length, next_a, next_ = early(right_rest, left_rest)
    groups = [
        (unit, norm, length, grad),
        (near_unit, near_norm, near_length, near),
        (next_unit, next_norm, next_length, next_),
    ]
    outs = [[((g[0].shape[0], texts_rest), BF16), ((g[0].shape[0], width), BF16)] for g in groups]
    texts_b, slopes_b, raw_grad, near_b, near_grad, next_b, next_grad = call(
        functools.partial(middle_kernel, 3),
        [((texts_rest, width), BF16), *itertools.chain(*outs)],
        [*itertools.chain(*groups), rest, text_y, *text_yc],
        24,
    )
    next_grad, far_low, far_high = lax.optimization_barrier((next_grad, far_low, far_high))
    share = (8, depth // 16, width)
    far_unit, far_a, far_b, mine, other = call(
        late_kernel,
        [unit_like, slopes_like, ((rows, texts_rest), BF16), (share, F32), (share, BF16)],
        [
            sensor_feats, right_low, left_high, right_rest, left_rest, far_low, far_high,
            raw_grad, near_grad, next_grad, proj_weight, texts_a, texts_b,
        ],
        24,
        scratch=[pltpu.VMEM((depth, 4 * rows), BF16)],
    )

    def text_sums(kernel, outs, mib, slopes, *others):
        operands = [unit, near_unit, next_unit, far_unit, *slopes, *others]
        return call(functools.partial(kernel, 4), outs, operands, mib)

    weight_recv = send(other, c=1)
    half_b = [slopes_b, near_b, next_b, far_b]
    away_b = text_sums(away_kernel, [grad_like], 20, half_b)[0]
    weight_recv, away_b = lax.optimization_barrier((weight_recv, away_b))
    weight_sum = call(add_kernel, [(share, BF16)], [mine, weight_recv], 12)[0]
    weight_all = lax.all_to_all(weight_sum, ("x", "yh"), split_axis=0, concat_axis=0, tiled=True)
    text_send, home_a, away_a = text_sums(
        home_kernel,
        [unit_like, grad_like, unit_like],
        58,
        [slopes_a, near_a, next_a, far_a, *half_b],
        send(away_b, c=1),
        text_y,
        text_feats,
        text_c,
    )
    text_out, away_a = send(text_send, yh=1), send(away_a, c=1)

    weight_sum = call(sum_kernel, [(share[1:], BF16)], [weight_all], 8)[0]
    across = send(weight_sum, z=2)
    ahead, behind = send(weight_sum, z=1), send(weight_sum, z=-1)
    home_a = call(add_text_kernel, [grad_like], [home_a, away_a], 12)[0]
    across, ahead, behind, home_a = lax.optimization_barrier((across, ahead, behind, home_a))
    weight_sum = (
        (weight_sum.astype(F32) + across.astype(F32)) + (ahead.astype(F32) + behind.astype(F32))
    ).astype(BF16)
    across = send(weight_sum, yl=1)
    text_grad = call(add_text_kernel, [grad_like], [home_a, text_out], 12)[0]
    across, text_grad = lax.optimization_barrier((across, text_grad))
    return (text_grad, weight_sum.astype(F32) + across.astype(F32))


def solution(mesh):
    fine = Mesh(mesh.devices.reshape(SIZES), AXES)
    return jax.shard_map(
        local,
        mesh=fine,
        in_specs=(P(AXES, None), P(), P(AXES, None)),
        out_specs=(P(AXES, None), P(("x", "yh", "c"), None)),
        check_vma=False,
    )
```
